32 devices in a mesh: img: 4 (over x, core), txt: 4 (over z), rep: 2 (over y).
Axes of the slice: x: 2, y: 2, z: 4, core: 2. Of those that a mesh axis runs over, the one named last changes fastest.
Arguments:
- images: bfloat16 [5120, 1152], P(('img', 'txt', 'rep'))
- texts: bfloat16 [5120, 1152], P(('txt', 'rep', 'img'))
- partner: int32 [5120], replicated, may hold values from 0 to 5119, as said below
- log_scale: float32 [1], replicated, may hold values from 2 to 2.5
- bias: float32 [1], replicated, may hold values from -8 to -6
Outputs:
- grad_images: float32 [5120, 1152], P(('img', 'txt', 'rep'))
- grad_texts: float32 [5120, 1152], P(('txt', 'rep', 'img'))
- scalars: float32 [3], replicated
The draws below stay inside these ranges and needn't reach their ends.
Inputs may be any that keep to these rules, and one draw needn't show every extreme that they name: partner[a] is the text row paired with image row a; every text row is named exactly once.
All inputs are finite; a program needn't handle non-finite values.
Results may differ from the reference program's by a relative error of at most 0.0039.
Values may be sent and summed in bfloat16 or wider, within the bound.
A program may use at most 128 MiB of HBM per device.

```python
import jax
import jax.numpy as jnp
from jax import lax

D = 1152
ROWS_DEV = 160
PAIRS = 5120
N_TXT = 4


def shared_draw(key):
    order = jax.random.permutation(jax.random.fold_in(key, 101), PAIRS).astype(jnp.int32)
    base = jax.random.normal(jax.random.fold_in(key, 102), (PAIRS, D), jnp.float32)
    return (order, base)


def draw_partner(key, part):
    order, base = shared_draw(key)
    return order


def draw_texts(key, part):
    low = 1.0
    high = 1.0
    order, base = shared_draw(key)
    key = jax.random.fold_in(key, 2)
    factor = jax.random.uniform(key, (PAIRS, 1), jnp.float32, jnp.log(low), jnp.log(high) + 0.001)
    return (base * jnp.exp(factor)).astype(jnp.bfloat16)


def draw_images(key, part):
    top = 2.0
    noise_width = 0.0
    order, base = shared_draw(key)
    key = jax.random.fold_in(key, 3)
    normal_noise = jax.random.normal(jax.random.fold_in(key, 1), (PAIRS, D), jnp.float32)
    flat_noise = jax.random.uniform(jax.random.fold_in(key, 2), (PAIRS, D), jnp.float32, -1.0, 1.0) * noise_width
    noise = jnp.where(noise_width > 0.0, flat_noise, normal_noise)
    position = jnp.arange(PAIRS, dtype=jnp.float32) / PAIRS
    jitter = jax.random.uniform(jax.random.fold_in(key, 4), (PAIRS,), jnp.float32, 0.7, 1.3)
    strength = 0.2 * jnp.exp(position * jnp.log(top / 0.2)) * jitter
    return (noise + strength[:, None] * base[order]).astype(jnp.bfloat16)


def setup_inputs(seed: int = 0) -> dict:
    key_of = jax.random.split(jax.random.key(seed), 6)
    return {
        "images": draw_images(jax.random.fold_in(key_of[5], 71), 0),
        "texts": draw_texts(jax.random.fold_in(key_of[5], 71), 0),
        "partner": draw_partner(jax.random.fold_in(key_of[5], 71), 0),
        "log_scale": jnp.clip(jax.random.uniform(key_of[3], (1,), jnp.float32, 2.0, 2.5), 2.0, 2.5),
        "bias": jnp.clip(jax.random.uniform(key_of[4], (1,), jnp.float32, -8.0, -6.0), -8.0, -6.0),
    }


def unit_rows(values):
    full = values.astype(jnp.float32)
    norm = jnp.sqrt(lax.optimization_barrier(jnp.sum(full * full, axis=1, keepdims=True)) + 1e-06)
    return (full / norm, norm)

def reference(images, texts, partner, log_scale, bias):
    img_unit, img_norm = unit_rows(images)
    txt_unit, txt_norm = unit_rows(texts)
    img_low = img_unit.astype(jnp.bfloat16)
    txt_low = txt_unit.astype(jnp.bfloat16)
    scale = jnp.exp(log_scale[0])
    shift = bias[0]
    span = ROWS_DEV * N_TXT
    count = PAIRS // span
    columns = jnp.arange(PAIRS, dtype=jnp.int32)

    def visit(carry, item):
        grad_txt, stats = carry
        rows_low, rows_partner = item
        sims = jnp.dot(rows_low, txt_low.T, preferred_element_type=jnp.float32)
        logits = scale * sims + shift
        positive = rows_partner[:, None] == columns[None, :]
        sign = jnp.where(positive, jnp.float32(1.0), jnp.float32(-1.0))
        margin = sign * logits
        pair_loss = jax.nn.softplus(-margin)
        slope = -sign * jax.nn.sigmoid(-margin)
        grad_tile = (scale * slope).astype(jnp.bfloat16)
        grad_rows = jnp.dot(grad_tile, txt_low, preferred_element_type=jnp.float32)
        grad_txt = grad_txt + jnp.dot(grad_tile.T, rows_low, preferred_element_type=jnp.float32)
        stats = stats + jnp.stack([jnp.sum(pair_loss), jnp.sum(slope * scale * sims), jnp.sum(slope)])
        return ((grad_txt, stats), grad_rows)
    start = (jnp.zeros((PAIRS, D), jnp.float32), jnp.zeros((3,), jnp.float32))
    blocks = (img_low.reshape(count, span, D), partner.reshape(count, span))
    (grad_txt_unit, stats), grad_img_unit = lax.scan(visit, start, blocks)
    grad_img_unit = grad_img_unit.reshape(PAIRS, D)
    grad_images = (grad_img_unit - img_unit * lax.optimization_barrier(jnp.sum(img_unit * grad_img_unit, axis=1, keepdims=True))) / img_norm
    grad_texts = (grad_txt_unit - txt_unit * lax.optimization_barrier(jnp.sum(txt_unit * grad_txt_unit, axis=1, keepdims=True))) / txt_norm
    scalars = stats / PAIRS
    return (grad_images, grad_texts, scalars)
```

```python
import functools

import jax
import jax.numpy as jnp
from jax import lax
from jax.experimental import pallas as pl
from jax.experimental.pallas import tpu as pltpu
from jax.sharding import PartitionSpec as P

MESH = pl.DeviceIdType.MESH
F32 = jnp.float32
BF16 = jnp.bfloat16
CHUNKS = 5


def row_norm(full):
    return jnp.sqrt(jnp.sum(full * full, axis=1, keepdims=True) + 1e-06)


def kernel(
    dims,
    images, texts, partner, log_scale, bias,
    out_img, out_txt, out_s,
    img_buf, txt_buf, gi, gt_own, gt_cs, gt_cr,
    gi_s1, gi_r1, gi_s2, gi_r2, gt_xs, gt_xr, gt_hs, gt_hr,
    stat_acc, st_buf,
    il_s, il_r, ir_s, ir_r, th_s, th_r, tx_s, tx_r, tc_s, tc_r,
    g1_s, g1_r, g2_s, g2_r, gc_s, gc_r, gx_s, gx_r, gh_s, gh_r, ss, sr,
):
    X, A, B, R = dims
    n_img, n_txt = 2 * X, A * B
    rows, width = images.shape
    crow = rows // CHUNKS
    i = lax.axis_index("img")
    t = lax.axis_index("txt")
    r = lax.axis_index("rep")
    x, c = i // 2, i % 2
    h, l = t // A, t % A
    other = 1 - c

    def rep_id(d):
        return {"rep": (r + d) % R}

    def lo_id(d):
        return {"txt": h * A + (l + d) % A}

    def hi_id(d):
        return {"txt": ((h + d) % B) * A + l}

    def x_id(d):
        return {"img": ((x + d) % X) * 2 + c}

    core_id = {"img": x * 2 + other}

    def signal(dev):
        pl.semaphore_signal(barrier, inc=1, device_id=dev, device_id_type=MESH)

    def copy(src, dst, send, recv, dev):
        return pltpu.make_async_remote_copy(
            src_ref=src, dst_ref=dst, send_sem=send, recv_sem=recv,
            device_id=dev, device_id_type=MESH,
        )

    barrier = pltpu.get_barrier_semaphore()
    peers = (
        [rep_id(d) for d in range(1, R)] + [lo_id(d) for d in range(1, A)]
        + [hi_id(d) for d in range(1, B)] + [x_id(d) for d in range(1, X)] + [core_id]
    )
    for dev in peers:
        signal(dev)

    def img_at(lp, rp, ch):
        return img_buf.at[pl.ds(pl.multiple_of((lp * R + rp) * rows + ch * crow, 16), crow)]

    def txt_at(hp, xp, cp, ch):
        return txt_buf.at[
            pl.ds(pl.multiple_of(((hp * X + xp) * 2 + cp) * rows + ch * crow, 16), crow)
        ]

    def img_lo(d, ch):
        return copy(img_at(l, r, ch), img_at(l, r, ch), il_s.at[d, ch], il_r.at[d, ch], lo_id(d))

    def img_rep(dl, d, ch):
        lp = (l + dl) % A
        ref = img_at(lp, r, ch)
        return copy(ref, ref, ir_s.at[dl, d, ch], ir_r.at[dl, d, ch], rep_id(d))

    def txt_hi(d, ch):
        ref = txt_at(h, x, c, ch)
        return copy(ref, ref, th_s.at[d, ch], th_r.at[d, ch], hi_id(d))

    def txt_x(dh, d, ch):
        ref = txt_at((h + dh) % B, x, c, ch)
        return copy(ref, ref, tx_s.at[dh, d, ch], tx_r.at[dh, d, ch], x_id(d))

    def txt_core(dh, dx, ch):
        ref = txt_at((h + dh) % B, (x + dx) % X, c, ch)
        return copy(ref, ref, tc_s.at[dh, dx, ch], tc_r.at[dh, dx, ch], core_id)

    full = images[...].astype(F32)
    img_norm = row_norm(full)
    img_buf[pl.ds(pl.multiple_of((l * R + r) * rows, 16), rows)] = (full / img_norm).astype(BF16)
    pl.semaphore_wait(barrier, len(peers))
    for ch in range(CHUNKS):
        for d in range(1, A):
            img_lo(d, ch).start()
        for d in range(1, R):
            img_rep(0, d, ch).start()
    full = texts[...].astype(F32)
    txt_norm = row_norm(full)
    txt_buf[pl.ds(pl.multiple_of(((h * X + x) * 2 + c) * rows, 16), rows)] = (
        full / txt_norm
    ).astype(BF16)
    for ch in range(CHUNKS):
        for d in range(1, B):
            txt_hi(d, ch).start()
        for d in range(1, X):
            txt_x(0, d, ch).start()
        txt_core(0, 0, ch).start()

    gi[...] = jnp.zeros_like(gi)
    stat_acc[...] = jnp.zeros_like(stat_acc)

    for ch in range(CHUNKS):
        for d in range(1, A):
            img_lo(d, ch).wait_recv()
            for e in range(1, R):
                img_rep(A - d, e, ch).start()
        for d in range(1, B):
            txt_hi(d, ch).wait_recv()
            for e in range(1, X):
                txt_x(B - d, e, ch).start()
            txt_core(B - d, 0, ch).start()
        for d in range(1, X):
            txt_x(0, d, ch).wait_recv()
            txt_core(0, X - d, ch).start()
    for ch in range(CHUNKS):
        for dh in range(1, B):
            for d in range(1, X):
                txt_x(dh, d, ch).wait_recv()
                txt_core(dh, X - d, ch).start()
    for ch in range(CHUNKS):
        for dl in range(A):
            for d in range(1, R):
                img_rep(dl, d, ch).wait_recv()

    scale = jnp.exp(jnp.full((8, 128), log_scale[0], F32))[:1, :1]
    shift = bias[0]
    group = A * R * rows
    lanes = group // 128
    first = (i * n_txt + h * A) * R * rows // 128
    wanted = [partner[pl.ds(first + k, 1), :] for k in range(lanes)]
    wanted = jnp.concatenate(wanted, axis=1)

    def grad_core(k):
        return copy(gt_cs.at[k], gt_cr.at[k], gc_s.at[k], gc_r.at[k], core_id)

    def grad_x(dx, dh, ch):
        part = pl.ds(pl.multiple_of(ch * crow, 16), crow)
        return copy(
            gt_xs.at[dx - 1, dh, part], gt_xr.at[dx - 1, dh, part],
            gx_s.at[dx - 1, dh, ch], gx_r.at[dx - 1, dh, ch], x_id(dx),
        )

    def finish(k):
        grad_core(k).wait_recv()
        dx = X - 1 - k // B
        dh = B - 1 - k % B

        @pl.when(dx > 0)
        def _():
            gt_xs[dx - 1, dh] = (gt_own[k] + gt_cr[k]).astype(BF16)
            for ch in range(CHUNKS):
                grad_x(dx, dh, ch).start()

    def step(k, _):
        dx = X - 1 - k // B
        dh = B - 1 - k % B
        hp, xp = (h + dh) % B, (x + dx) % X
        for ch in range(CHUNKS):
            txt_core(dh, dx, ch).wait_recv()
        base = pl.multiple_of((hp * X + xp) * 2 * rows, 16)
        block = txt_buf[pl.ds(base, 2 * rows)]
        all_img = img_buf[...]
        sims = lax.dot_general(
            block, all_img, (((1,), (1,)), ((), ())), preferred_element_type=F32
        )
        start = ((hp * A + l) * R + r) * n_img * rows + xp * 2 * rows
        ids = start + lax.broadcasted_iota(jnp.int32, sims.shape, 0)
        positive = ids == wanted
        scaled = scale * sims
        logits = scaled + shift
        margin = jnp.where(positive, logits, -logits)
        e = jnp.exp(-jnp.abs(margin))
        u = 1.0 + e
        inv = 1.0 / u
        loss = jnp.maximum(-margin, 0.0) + (jnp.log(u) + (e - (u - 1.0)) * inv)
        sig = jnp.where(margin >= 0.0, e, 1.0) * inv
        slope = jnp.where(positive, -sig, sig)
        grad = (scale * slope).astype(BF16)
        stat_acc[0:1, :] += jnp.sum(loss, axis=0, keepdims=True)
        stat_acc[1:2, :] += jnp.sum(slope * scaled, axis=0, keepdims=True)
        stat_acc[2:3, :] += jnp.sum(slope, axis=0, keepdims=True)
        g_txt = jnp.dot(grad, all_img, preferred_element_type=F32)
        mine = c == 0
        gt_cs[k] = jnp.where(mine, g_txt[rows:], g_txt[:rows])
        grad_core(k).start()
        gt_own[k] = jnp.where(mine, g_txt[:rows], g_txt[rows:])
        gi[...] += lax.dot_general(
            grad, block, (((0,), (0,)), ((), ())), preferred_element_type=F32
        )

        @pl.when(k > 0)
        def _():
            finish(k - 1)

        return 0

    lax.fori_loop(0, B * X, step, 0)

    def gi_at(dl, d, ch):
        lp, rp = (l + dl) % A, (r + d) % R
        return pl.ds(pl.multiple_of((lp * R + rp) * rows + ch * crow, 16), crow)

    def cut(ch):
        return pl.ds(ch * crow, crow)

    def grad_rep(d, dl, ch):
        return copy(
            gi_s1.at[d - 1, dl, cut(ch)], gi_r1.at[d - 1, dl, cut(ch)],
            g1_s.at[d - 1, dl, ch], g1_r.at[d - 1, dl, ch], rep_id(d),
        )

    def grad_lo(d, ch):
        return copy(
            gi_s2.at[d - 1, cut(ch)], gi_r2.at[d - 1, cut(ch)],
            g2_s.at[d - 1, ch], g2_r.at[d - 1, ch], lo_id(d),
        )

    def grad_hi(d, ch):
        return copy(
            gt_hs.at[d - 1, cut(ch)], gt_hr.at[d - 1, cut(ch)],
            gh_s.at[d - 1, ch], gh_r.at[d - 1, ch], hi_id(d),
        )

    for dl in list(range(1, A)) + [0]:
        for d in range(1, R):
            for ch in range(CHUNKS):
                gi_s1[d - 1, dl, cut(ch)] = gi[gi_at(dl, d, ch)].astype(BF16)
                grad_rep(d, dl, ch).start()
    finish(B * X - 1)

    st_axes = [
        (2, c, lambda d: core_id), (X, x, x_id), (R, r, rep_id), (B, h, hi_id), (A, l, lo_id),
    ]
    value = stat_acc[:, 0:128]
    for k in range(1, lanes):
        value = value + stat_acc[:, k * 128:(k + 1) * 128]

    def stat_copy(stage, d):
        size, at, ident = st_axes[stage]
        return copy(
            st_buf.at[stage, at], st_buf.at[stage, at], ss.at[stage, d], sr.at[stage, d], ident(d)
        )

    def stat_start(stage, value):
        st_buf[stage, st_axes[stage][1]] = value
        for d in range(1, st_axes[stage][0]):
            stat_copy(stage, d).start()

    def stat_end(stage):
        size = st_axes[stage][0]
        for d in range(1, size):
            stat_copy(stage, d).wait_recv()
        total = st_buf[stage, 0]
        for k in range(1, size):
            total = total + st_buf[stage, k]
        return total

    stat_start(0, value)
    value = stat_end(0)
    stat_start(1, value)

    def own_txt(dh, ch):
        k = B * (X - 1) + (B - 1 - dh)
        return gt_own[k, cut(ch)] + gt_cr[k, cut(ch)]

    for ch in range(CHUNKS):
        for dh in range(1, B):
            total = own_txt(dh, ch)
            for d in range(1, X):
                grad_x(d, dh, ch).wait_recv()
                total = total + gt_xr[d - 1, dh, cut(ch)].astype(F32)
            gt_hs[dh - 1, cut(ch)] = total.astype(BF16)
            grad_hi(dh, ch).start()
        for dl in range(1, A):
            total = gi[gi_at(dl, 0, ch)]
            for d in range(1, R):
                grad_rep(d, dl, ch).wait_recv()
                total = total + gi_r1[d - 1, dl, cut(ch)].astype(F32)
            gi_s2[dl - 1, cut(ch)] = total.astype(BF16)
            grad_lo(dl, ch).start()

    for stage in range(1, 4):
        value = stat_end(stage)
        stat_start(stage + 1, value)

    for ch in range(CHUNKS):
        part = cut(ch)
        total = own_txt(0, ch)
        for d in range(1, X):
            grad_x(d, 0, ch).wait_recv()
            total = total + gt_xr[d - 1, 0, part].astype(F32)
        for d in range(1, B):
            grad_hi(d, ch).wait_recv()
            total = total + gt_hr[d - 1, part].astype(F32)
        norm = txt_norm[ch * crow:(ch + 1) * crow]
        unit = texts[part].astype(F32) / norm
        along = jnp.sum(unit * total, axis=1, keepdims=True)
        out_txt[part] = (total - unit * along) / norm

        total = gi[gi_at(0, 0, ch)]
        for d in range(1, R):
            grad_rep(d, 0, ch).wait_recv()
            total = total + gi_r1[d - 1, 0, part].astype(F32)
        for d in range(1, A):
            grad_lo(d, ch).wait_recv()
            total = total + gi_r2[d - 1, part].astype(F32)
        norm = img_norm[ch * crow:(ch + 1) * crow]
        unit = images[part].astype(F32) / norm
        along = jnp.sum(unit * total, axis=1, keepdims=True)
        out_img[part] = (total - unit * along) / norm

    value = stat_end(4)
    pairs = rows * n_img * n_txt * R
    for k in range(3):
        out_s[k] = jnp.sum(value[k:k + 1, :]) / pairs

    for ch in range(CHUNKS):
        for d in range(1, A):
            img_lo(d, ch).wait_send()
            grad_lo(d, ch).wait_send()
        for d in range(1, R):
            for dl in range(A):
                img_rep(dl, d, ch).wait_send()
                grad_rep(d, dl, ch).wait_send()
        for d in range(1, B):
            txt_hi(d, ch).wait_send()
            grad_hi(d, ch).wait_send()
        for dh in range(B):
            for d in range(1, X):
                txt_x(dh, d, ch).wait_send()
                grad_x(d, dh, ch).wait_send()
            for dx in range(X):
                txt_core(dh, dx, ch).wait_send()
    for k in range(B * X):
        grad_core(k).wait_send()
    for stage in range(5):
        for d in range(1, st_axes[stage][0]):
            stat_copy(stage, d).wait_send()


def on_device(dims, images, texts, partner, log_scale, bias):
    X, A, B, R = dims
    rows, width = images.shape
    group = A * R * rows
    nt = B * X
    most = max(2, X, A, B, R)
    dma = pltpu.SemaphoreType.DMA
    vm = pl.BlockSpec(memory_space=pltpu.VMEM)
    sm = pl.BlockSpec(memory_space=pltpu.SMEM)
    C = CHUNKS
    return pl.pallas_call(
        functools.partial(kernel, dims),
        out_shape=(
            jax.ShapeDtypeStruct((rows, width), F32),
            jax.ShapeDtypeStruct((rows, width), F32),
            jax.ShapeDtypeStruct((3,), F32),
        ),
        in_specs=[vm, vm, vm, sm, sm],
        out_specs=(vm, vm, sm),
        scratch_shapes=[
            pltpu.VMEM((group, width), BF16),
            pltpu.VMEM((nt * 2 * rows, width), BF16),
            pltpu.VMEM((group, width), F32),
            pltpu.VMEM((nt, rows, width), F32),
            pltpu.VMEM((nt, rows, width), F32),
            pltpu.VMEM((nt, rows, width), F32),
            pltpu.VMEM((R - 1, A, rows, width), BF16),
            pltpu.VMEM((R - 1, A, rows, width), BF16),
            pltpu.VMEM((A - 1, rows, width), BF16),
            pltpu.VMEM((A - 1, rows, width), BF16),
            pltpu.VMEM((X - 1, B, rows, width), BF16),
            pltpu.VMEM((X - 1, B, rows, width), BF16),
            pltpu.VMEM((B - 1, rows, width), BF16),
            pltpu.VMEM((B - 1, rows, width), BF16),
            pltpu.VMEM((8, group), F32),
            pltpu.VMEM((5, most, 8, 128), F32),
            dma((A, C)), dma((A, C)), dma((A, R, C)), dma((A, R, C)),
            dma((B, C)), dma((B, C)), dma((B, X, C)), dma((B, X, C)),
            dma((B, X, C)), dma((B, X, C)),
            dma((R - 1, A, C)), dma((R - 1, A, C)), dma((A - 1, C)), dma((A - 1, C)),
            dma((nt,)), dma((nt,)),
            dma((X - 1, B, C)), dma((X - 1, B, C)), dma((B - 1, C)), dma((B - 1, C)),
            dma((5, most)), dma((5, most)),
        ],
        compiler_params=pltpu.CompilerParams(
            collective_id=0, has_side_effects=True, vmem_limit_bytes=60 * 2**20
        ),
    )(images, texts, partner.reshape(-1, 128), log_scale, bias)


def solution(mesh):
    n_img, n_txt, n_rep = mesh.shape["img"], mesh.shape["txt"], mesh.shape["rep"]
    dims = (n_img // 2, n_txt // 2, 2, n_rep)
    in_specs = (P(("img", "txt", "rep"), None), P(("txt", "rep", "img"), None), P(), P(), P())
    out_specs = (P(("img", "txt", "rep"), None), P(("txt", "rep", "img"), None), P())
    return jax.shard_map(
        functools.partial(on_device, dims), mesh=mesh,
        in_specs=in_specs, out_specs=out_specs, check_vma=False,
    )
```

```python
import functools

import jax
import jax.numpy as jnp
from jax import lax
from jax.experimental import pallas as pl
from jax.experimental.pallas import tpu as pltpu
from jax.sharding import PartitionSpec as P

MESH = pl.DeviceIdType.MESH
F32 = jnp.float32
BF16 = jnp.bfloat16
CHUNKS = 5


def row_norm(full):
    return jnp.sqrt(jnp.sum(full * full, axis=1, keepdims=True) + 1e-06)


def kernel(
    dims,
    images, texts, partner, log_scale, bias,
    out_img, out_txt, out_s,
    img_buf, txt_buf, gi, gt_own, gt_cs, gt_cr,
    gi_s1, gi_r1, gi_s2, gi_r2, gt_xs, gt_xr, gt_hs, gt_hr,
    stat_acc, st_buf,
    il_s, il_r, ir_s, ir_r, th_s, th_r, tx_s, tx_r, tc_s, tc_r,
    g1_s, g1_r, g2_s, g2_r, gc_s, gc_r, gx_s, gx_r, gh_s, gh_r, ss, sr,
):
    X, A, B, R = dims
    n_img, n_txt = 2 * X, A * B
    rows, width = images.shape
    crow = rows // CHUNKS
    i = lax.axis_index("img")
    t = lax.axis_index("txt")
    r = lax.axis_index("rep")
    x, c = i // 2, i % 2
    h, l = t // A, t % A
    other = 1 - c

    def rep_id(d):
        return {"rep": (r + d) % R}

    def lo_id(d):
        return {"txt": h * A + (l + d) % A}

    def hi_id(d):
        return {"txt": ((h + d) % B) * A + l}

    def x_id(d):
        return {"img": ((x + d) % X) * 2 + c}

    def img_id(d):
        return {"img": (i + d) % n_img}

    def txt_id(d):
        return {"txt": (t + d) % n_txt}

    core_id = {"img": x * 2 + other}

    def signal(dev):
        pl.semaphore_signal(barrier, inc=1, device_id=dev, device_id_type=MESH)

    def copy(src, dst, send, recv, dev):
        return pltpu.make_async_remote_copy(
            src_ref=src, dst_ref=dst, send_sem=send, recv_sem=recv,
            device_id=dev, device_id_type=MESH,
        )

    barrier = pltpu.get_barrier_semaphore()
    peers = (
        [rep_id(d) for d in range(1, R)] + [img_id(d) for d in range(1, n_img)]
        + [txt_id(d) for d in range(1, n_txt)]
    )
    for dev in peers:
        signal(dev)

    def img_at(lp, rp, ch):
        return img_buf.at[pl.ds(pl.multiple_of((lp * R + rp) * rows + ch * crow, 16), crow)]

    def txt_at(hp, xp, cp, ch):
        return txt_buf.at[
            pl.ds(pl.multiple_of(((hp * X + xp) * 2 + cp) * rows + ch * crow, 16), crow)
        ]

    def img_lo(d, ch):
        return copy(img_at(l, r, ch), img_at(l, r, ch), il_s.at[d, ch], il_r.at[d, ch], lo_id(d))

    def img_rep(dl, d, ch):
        lp = (l + dl) % A
        ref = img_at(lp, r, ch)
        return copy(ref, ref, ir_s.at[dl, d, ch], ir_r.at[dl, d, ch], rep_id(d))

    def txt_hi(d, ch):
        ref = txt_at(h, x, c, ch)
        return copy(ref, ref, th_s.at[d, ch], th_r.at[d, ch], hi_id(d))

    def txt_x(dh, d, ch):
        ref = txt_at((h + dh) % B, x, c, ch)
        return copy(ref, ref, tx_s.at[dh, d, ch], tx_r.at[dh, d, ch], x_id(d))

    def txt_core(dh, dx, ch):
        ref = txt_at((h + dh) % B, (x + dx) % X, c, ch)
        return copy(ref, ref, tc_s.at[dh, dx, ch], tc_r.at[dh, dx, ch], core_id)

    full = images[...].astype(F32)
    img_norm = row_norm(full)
    img_buf[pl.ds(pl.multiple_of((l * R + r) * rows, 16), rows)] = (full / img_norm).astype(BF16)
    pl.semaphore_wait(barrier, len(peers))
    for ch in range(CHUNKS):
        for d in range(1, A):
            img_lo(d, ch).start()
        for d in range(1, R):
            img_rep(0, d, ch).start()
    full = texts[...].astype(F32)
    txt_norm = row_norm(full)
    txt_buf[pl.ds(pl.multiple_of(((h * X + x) * 2 + c) * rows, 16), rows)] = (
        full / txt_norm
    ).astype(BF16)
    for ch in range(CHUNKS):
        for d in range(1, B):
            txt_hi(d, ch).start()
        for d in range(1, X):
            txt_x(0, d, ch).start()
        txt_core(0, 0, ch).start()

    gi[...] = jnp.zeros_like(gi)
    stat_acc[...] = jnp.zeros_like(stat_acc)

    for ch in range(CHUNKS):
        for d in range(1, A):
            img_lo(d, ch).wait_recv()
            for e in range(1, R):
                img_rep(A - d, e, ch).start()
        for d in range(1, B):
            txt_hi(d, ch).wait_recv()
            for e in range(1, X):
                txt_x(B - d, e, ch).start()
            txt_core(B - d, 0, ch).start()
        for d in range(1, X):
            txt_x(0, d, ch).wait_recv()
            txt_core(0, X - d, ch).start()
    for ch in range(CHUNKS):
        for dh in range(1, B):
            for d in range(1, X):
                txt_x(dh, d, ch).wait_recv()
                txt_core(dh, X - d, ch).start()
    for ch in range(CHUNKS):
        for dl in range(A):
            for d in range(1, R):
                img_rep(dl, d, ch).wait_recv()

    scale = jnp.exp(jnp.full((8, 128), log_scale[0], F32))[:1, :1]
    shift = bias[0]
    group = A * R * rows
    lanes = group // 128
    first = (i * n_txt + h * A) * R * rows // 128
    wanted = [partner[pl.ds(first + k, 1), :] for k in range(lanes)]
    wanted = jnp.concatenate(wanted, axis=1)

    def grad_core(k):
        return copy(gt_cs.at[k], gt_cr.at[k], gc_s.at[k], gc_r.at[k], core_id)

    def grad_x(dx, dh, ch):
        part = pl.ds(pl.multiple_of(ch * crow, 16), crow)
        return copy(
            gt_xs.at[dx - 1, dh, part], gt_xr.at[dx - 1, dh, part],
            gx_s.at[dx - 1, dh, ch], gx_r.at[dx - 1, dh, ch], x_id(dx),
        )

    def finish(k):
        grad_core(k).wait_recv()
        dx = X - 1 - k // B
        dh = B - 1 - k % B

        @pl.when(dx > 0)
        def _():
            gt_xs[dx - 1, dh] = (gt_own[k] + gt_cr[k]).astype(BF16)
            for ch in range(CHUNKS):
                grad_x(dx, dh, ch).start()

    def step(k, _):
        dx = X - 1 - k // B
        dh = B - 1 - k % B
        hp, xp = (h + dh) % B, (x + dx) % X
        for ch in range(CHUNKS):
            txt_core(dh, dx, ch).wait_recv()
        base = pl.multiple_of((hp * X + xp) * 2 * rows, 16)
        block = txt_buf[pl.ds(base, 2 * rows)]
        all_img = img_buf[...]
        sims = lax.dot_general(
            block, all_img, (((1,), (1,)), ((), ())), preferred_element_type=F32
        )
        start = ((hp * A + l) * R + r) * n_img * rows + xp * 2 * rows
        ids = start + lax.broadcasted_iota(jnp.int32, sims.shape, 0)
        positive = ids == wanted
        scaled = scale * sims
        logits = scaled + shift
        margin = jnp.where(positive, logits, -logits)
        e = jnp.exp(-jnp.abs(margin))
        u = 1.0 + e
        inv = 1.0 / u
        loss = jnp.maximum(-margin, 0.0) + (jnp.log(u) + (e - (u - 1.0)) * inv)
        sig = jnp.where(margin >= 0.0, e, 1.0) * inv
        slope = jnp.where(positive, -sig, sig)
        grad = (scale * slope).astype(BF16)
        stat_acc[0:1, :] += jnp.sum(loss, axis=0, keepdims=True)
        stat_acc[1:2, :] += jnp.sum(slope * scaled, axis=0, keepdims=True)
        stat_acc[2:3, :] += jnp.sum(slope, axis=0, keepdims=True)
        g_txt = jnp.dot(grad, all_img, preferred_element_type=F32)
        mine = c == 0
        gt_cs[k] = jnp.where(mine, g_txt[rows:], g_txt[:rows])
        grad_core(k).start()
        gt_own[k] = jnp.where(mine, g_txt[:rows], g_txt[rows:])
        gi[...] += lax.dot_general(
            grad, block, (((0,), (0,)), ((), ())), preferred_element_type=F32
        )

        @pl.when(k > 0)
        def _():
            finish(k - 1)

        return 0

    lax.fori_loop(0, B * X, step, 0)

    def gi_at(dl, d, ch):
        lp, rp = (l + dl) % A, (r + d) % R
        return pl.ds(pl.multiple_of((lp * R + rp) * rows + ch * crow, 16), crow)

    def cut(ch):
        return pl.ds(ch * crow, crow)

    def grad_rep(d, dl, ch):
        return copy(
            gi_s1.at[d - 1, dl, cut(ch)], gi_r1.at[d - 1, dl, cut(ch)],
            g1_s.at[d - 1, dl, ch], g1_r.at[d - 1, dl, ch], rep_id(d),
        )

    def grad_lo(d, ch):
        return copy(
            gi_s2.at[d - 1, cut(ch)], gi_r2.at[d - 1, cut(ch)],
            g2_s.at[d - 1, ch], g2_r.at[d - 1, ch], lo_id(d),
        )

    def grad_hi(d, ch):
        return copy(
            gt_hs.at[d - 1, cut(ch)], gt_hr.at[d - 1, cut(ch)],
            gh_s.at[d - 1, ch], gh_r.at[d - 1, ch], hi_id(d),
        )

    st_axes = [(R, r, rep_id), (n_txt, t, txt_id), (n_img, i, img_id)]

    def stat_copy(stage, d):
        size, at, ident = st_axes[stage]
        return copy(
            st_buf.at[stage, at], st_buf.at[stage, at], ss.at[stage, d], sr.at[stage, d], ident(d)
        )

    def stat_start(stage, value):
        st_buf[stage, st_axes[stage][1]] = value
        for d in range(1, st_axes[stage][0]):
            stat_copy(stage, d).start()

    def stat_end(stage):
        size = st_axes[stage][0]
        for d in range(1, size):
            stat_copy(stage, d).wait_recv()
        total = st_buf[stage, 0]
        for k in range(1, size):
            total = total + st_buf[stage, k]
        return total

    value = stat_acc[:, 0:128]
    for k in range(1, lanes):
        value = value + stat_acc[:, k * 128:(k + 1) * 128]
    stat_start(0, value)

    for dl in list(range(1, A)) + [0]:
        for d in range(1, R):
            for ch in range(CHUNKS):
                gi_s1[d - 1, dl, cut(ch)] = gi[gi_at(dl, d, ch)].astype(BF16)
                grad_rep(d, dl, ch).start()
    finish(B * X - 1)
    stat_start(1, stat_end(0))

    def own_txt(dh, ch):
        k = B * (X - 1) + (B - 1 - dh)
        return gt_own[k, cut(ch)] + gt_cr[k, cut(ch)]

    for ch in range(CHUNKS):
        for dh in range(1, B):
            total = own_txt(dh, ch)
            for d in range(1, X):
                grad_x(d, dh, ch).wait_recv()
                total = total + gt_xr[d - 1, dh, cut(ch)].astype(F32)
            gt_hs[dh - 1, cut(ch)] = total.astype(BF16)
            grad_hi(dh, ch).start()
        for dl in range(1, A):
            total = gi[gi_at(dl, 0, ch)]
            for d in range(1, R):
                grad_rep(d, dl, ch).wait_recv()
                total = total + gi_r1[d - 1, dl, cut(ch)].astype(F32)
            gi_s2[dl - 1, cut(ch)] = total.astype(BF16)
            grad_lo(dl, ch).start()

    stat_start(2, stat_end(1))

    for ch in range(CHUNKS):
        part = cut(ch)
        total = own_txt(0, ch)
        for d in range(1, X):
            grad_x(d, 0, ch).wait_recv()
            total = total + gt_xr[d - 1, 0, part].astype(F32)
        for d in range(1, B):
            grad_hi(d, ch).wait_recv()
            total = total + gt_hr[d - 1, part].astype(F32)
        norm = txt_norm[ch * crow:(ch + 1) * crow]
        unit = texts[part].astype(F32) / norm
        along = jnp.sum(unit * total, axis=1, keepdims=True)
        out_txt[part] = (total - unit * along) / norm

        total = gi[gi_at(0, 0, ch)]
        for d in range(1, R):
            grad_rep(d, 0, ch).wait_recv()
            total = total + gi_r1[d - 1, 0, part].astype(F32)
        for d in range(1, A):
            grad_lo(d, ch).wait_recv()
            total = total + gi_r2[d - 1, part].astype(F32)
        norm = img_norm[ch * crow:(ch + 1) * crow]
        unit = images[part].astype(F32) / norm
        along = jnp.sum(unit * total, axis=1, keepdims=True)
        out_img[part] = (total - unit * along) / norm

    value = stat_end(2)
    pairs = rows * n_img * n_txt * R
    for k in range(3):
        out_s[k] = jnp.sum(value[k:k + 1, :]) / pairs

    for ch in range(CHUNKS):
        for d in range(1, A):
            img_lo(d, ch).wait_send()
            grad_lo(d, ch).wait_send()
        for d in range(1, R):
            for dl in range(A):
                img_rep(dl, d, ch).wait_send()
                grad_rep(d, dl, ch).wait_send()
        for d in range(1, B):
            txt_hi(d, ch).wait_send()
            grad_hi(d, ch).wait_send()
        for dh in range(B):
            for d in range(1, X):
                txt_x(dh, d, ch).wait_send()
                grad_x(d, dh, ch).wait_send()
            for dx in range(X):
                txt_core(dh, dx, ch).wait_send()
    for k in range(B * X):
        grad_core(k).wait_send()
    for stage in range(3):
        for d in range(1, st_axes[stage][0]):
            stat_copy(stage, d).wait_send()


def on_device(dims, images, texts, partner, log_scale, bias):
    X, A, B, R = dims
    rows, width = images.shape
    group = A * R * rows
    nt = B * X
    most = max(2 * X, A * B, R)
    dma = pltpu.SemaphoreType.DMA
    vm = pl.BlockSpec(memory_space=pltpu.VMEM)
    sm = pl.BlockSpec(memory_space=pltpu.SMEM)
    C = CHUNKS
    return pl.pallas_call(
        functools.partial(kernel, dims),
        out_shape=(
            jax.ShapeDtypeStruct((rows, width), F32),
            jax.ShapeDtypeStruct((rows, width), F32),
            jax.ShapeDtypeStruct((3,), F32),
        ),
        in_specs=[vm, vm, vm, sm, sm],
        out_specs=(vm, vm, sm),
        scratch_shapes=[
            pltpu.VMEM((group, width), BF16),
            pltpu.VMEM((nt * 2 * rows, width), BF16),
            pltpu.VMEM((group, width), F32),
            pltpu.VMEM((nt, rows, width), F32),
            pltpu.VMEM((nt, rows, width), F32),
            pltpu.VMEM((nt, rows, width), F32),
            pltpu.VMEM((R - 1, A, rows, width), BF16),
            pltpu.VMEM((R - 1, A, rows, width), BF16),
            pltpu.VMEM((A - 1, rows, width), BF16),
            pltpu.VMEM((A - 1, rows, width), BF16),
            pltpu.VMEM((X - 1, B, rows, width), BF16),
            pltpu.VMEM((X - 1, B, rows, width), BF16),
            pltpu.VMEM((B - 1, rows, width), BF16),
            pltpu.VMEM((B - 1, rows, width), BF16),
            pltpu.VMEM((8, group), F32),
            pltpu.VMEM((3, most, 8, 128), F32),
            dma((A, C)), dma((A, C)), dma((A, R, C)), dma((A, R, C)),
            dma((B, C)), dma((B, C)), dma((B, X, C)), dma((B, X, C)),
            dma((B, X, C)), dma((B, X, C)),
            dma((R - 1, A, C)), dma((R - 1, A, C)), dma((A - 1, C)), dma((A - 1, C)),
            dma((nt,)), dma((nt,)),
            dma((X - 1, B, C)), dma((X - 1, B, C)), dma((B - 1, C)), dma((B - 1, C)),
            dma((3, most)), dma((3, most)),
        ],
        compiler_params=pltpu.CompilerParams(
            collective_id=0, has_side_effects=True, vmem_limit_bytes=60 * 2**20
        ),
    )(images, texts, partner.reshape(-1, 128), log_scale, bias)


def solution(mesh):
    n_img, n_txt, n_rep = mesh.shape["img"], mesh.shape["txt"], mesh.shape["rep"]
    dims = (n_img // 2, n_txt // 2, 2, n_rep)
    in_specs = (P(("img", "txt", "rep"), None), P(("txt", "rep", "img"), None), P(), P(), P())
    out_specs = (P(("img", "txt", "rep"), None), P(("txt", "rep", "img"), None), P())
    return jax.shard_map(
        functools.partial(on_device, dims), mesh=mesh,
        in_specs=in_specs, out_specs=out_specs, check_vma=False,
    )
```
